256 devices in a mesh: expert: 32 (over x_lo, z, core), dp: 8 (over x_hi, y).
Axes of the slice: x: 4 (x_hi: 2, x_lo: 2; x = x_hi * 2 + x_lo), y: 4, z: 8, core: 2. Of those that a mesh axis runs over, the one named last changes fastest.
Arguments:
- tokens: bfloat16 [16384, 2048], P(('expert', 'dp')), may hold values from -6 to 6
- expert_ids: int32 [16384, 2], P(('expert', 'dp')), may hold values from 0 to 31, as said below
- gate_codes: int32 [16384, 2], P(('expert', 'dp')), may hold values from 1 to 4095
- expert_order: int32 [32], replicated, may hold values from 0 to 31, each once
- w_gate: bfloat16 [32, 2048, 7168], P('expert', None, 'dp'), may hold values from -0.125 to 0.125
- w_up: bfloat16 [32, 2048, 7168], P('expert', None, 'dp'), may hold values from -0.125 to 0.125
- w_down: bfloat16 [32, 7168, 2048], P('expert', 'dp'), may hold values from -0.0625 to 0.0625
Outputs:
- mixed: bfloat16 [16384, 2048], P(('expert', 'dp'))
The draws below stay inside these ranges and needn't reach their ends.
Inputs may be any that keep to these rules, and one draw needn't show every extreme that they name: `expert_ids`: in each aligned block of 64 tokens (the tokens of one device), every id below 2 is named by exactly 8 tokens, and every other id by at most 4 tokens, some of them by exactly 4. A token's two ids differ. `expert_order`: each expert number appears once.
All inputs are finite; a program needn't handle non-finite values.
Results may differ from the reference program's by a relative error of at most 0.017.
Values may be sent and summed in bfloat16 or wider, within the bound.
No kernel may reach another device: no remote copies, remote signals or barrier semaphores. Data moves between devices by JAX's collectives and lax.ppermute only.
A program may use at most 128 MiB of HBM per device.

```python
import jax
import jax.numpy as jnp
from jax import lax

D = 2048
FF = 7168
HOT = 2
TOK_DEV = 64
EXPERTS = 32
TOKENS = 16384
HOT_ROWS = 8
NCOLD = 30
COLD = 112
CAP = 8
N_EXPERT = 32
N_DP = 8


def draw_expert_ids(key, part):
    block_keys = jax.random.split(jax.random.fold_in(key, 11), TOKENS // TOK_DEV)
    hot_span = HOT * HOT_ROWS

    def one_block(block_key):
        block_parts = jax.random.split(block_key, 4)
        cold_order = HOT + jax.random.permutation(block_parts[0], NCOLD).astype(jnp.int32)
        offset = jax.random.randint(block_parts[1], (), 0, NCOLD)
        slot_expert = cold_order[(jnp.arange(COLD) + offset) % NCOLD]
        token_place = jnp.arange(TOK_DEV)
        pair_slot = hot_span + 2 * (token_place - hot_span)
        hot_id = jnp.minimum(token_place // HOT_ROWS, HOT - 1).astype(jnp.int32)
        first_id = jnp.where(token_place < hot_span, hot_id, slot_expert[jnp.clip(pair_slot, 0, COLD - 1)])
        second_id = jnp.where(token_place < hot_span, slot_expert[jnp.clip(token_place, 0, COLD - 1)], slot_expert[jnp.clip(pair_slot + 1, 0, COLD - 1)])
        pair_ids = jnp.stack([first_id, second_id], axis=-1)
        flipped = jax.random.randint(block_parts[2], (TOK_DEV,), 0, 2)
        pair_ids = jnp.where(flipped[:, None] == 1, pair_ids[:, ::-1], pair_ids)
        shuffle = jax.random.permutation(block_parts[3], TOK_DEV)
        return pair_ids[shuffle]
    return jax.vmap(one_block)(block_keys).reshape(TOKENS, 2).astype(jnp.int32)


def plant(drawn, stream_key, smallest, largest):
    extent = drawn.shape
    index_at = [jax.random.randint(jax.random.fold_in(stream_key, axis), (), 0, extent[axis]) for axis in range(len(extent))]
    drawn = drawn.at[tuple(index_at)].set(smallest)
    longest = extent.index(max(extent))
    index_at[longest] = (index_at[longest] + 1) % extent[longest]
    return drawn.at[tuple(index_at)].set(largest)


def level_of(own_key, dims, cuts, smallest, largest):
    def one(position, blocks):
        steps = jax.random.uniform(jax.random.fold_in(jax.random.fold_in(own_key, 6), position), (blocks,), jnp.float32, smallest / len(cuts), largest / len(cuts))
        return jnp.repeat(jnp.exp(steps), dims[position] // blocks).reshape((-1,) + (1,) * (len(dims) - position - 1))

    level = one(*cuts[0])
    for cut in cuts[1:]:
        level = level * one(*cut)
    return level


def normal_values(stream_key, shape, spread, reach, shards=(), kind=jnp.bfloat16):
    values = jax.random.normal(stream_key, shape, jnp.float32) * spread
    if len(shards) > 0:
        values = level_of(stream_key, shape, shards, -0.22, 0.18) * values
    return jnp.clip(values, min=-reach, max=reach).astype(kind)


def setup_inputs(seed: int = 0) -> dict:
    seeds = jax.random.split(jax.random.key(seed), 8)
    tokens = normal_values(seeds[0], (TOKENS, D), 1.0, 6.0, ((0, 256),))
    expert_ids = draw_expert_ids(jax.random.fold_in(seeds[7], 71), 0)
    gate_codes = plant(jax.random.randint(seeds[2], (TOKENS, 2), 1, 4096), jax.random.fold_in(seeds[2], 1), 1, 4095).astype(jnp.int32)
    expert_order = jax.random.permutation(seeds[3], EXPERTS).astype(jnp.int32)
    w_gate = normal_values(seeds[4], (EXPERTS, D, FF), D ** -0.5, 0.125, ((0, 32), (2, 8)))
    w_up = normal_values(seeds[5], (EXPERTS, D, FF), D ** -0.5, 0.125, ((0, 32), (2, 8)))
    w_down = normal_values(seeds[6], (EXPERTS, FF, D), FF ** -0.5, 0.0625, ((0, 32), (1, 8)))
    return dict(tokens=tokens, expert_ids=expert_ids, gate_codes=gate_codes, expert_order=expert_order, w_gate=w_gate, w_up=w_up, w_down=w_down)


def expert_forward(token_rows, gate_matrix, up_matrix, down_matrix):
    gate_value = jnp.dot(token_rows, gate_matrix, preferred_element_type=jnp.float32)
    up_value = jnp.dot(token_rows, up_matrix, preferred_element_type=jnp.float32)
    hidden = (jax.nn.silu(gate_value) * up_value).astype(jnp.bfloat16)
    row_total = hidden.shape[0]
    block_units = FF // N_DP
    hidden_blocks = hidden.reshape(row_total, N_DP, block_units).astype(jnp.float32)
    down_blocks = down_matrix.reshape(N_DP, block_units, D).astype(jnp.float32)
    partial_value = jnp.einsum("rnf,nfd->nrd", hidden_blocks, down_blocks).astype(jnp.bfloat16)
    partial_value = lax.optimization_barrier(partial_value)
    return jnp.sum(partial_value.astype(jnp.float32), axis=0).astype(jnp.bfloat16)


def reference(tokens, expert_ids, gate_codes, expert_order, w_gate, w_up, w_down):
    physical = expert_order[expert_ids].reshape(-1).astype(jnp.int32)
    total_rows = physical.shape[0]
    repeated = jnp.repeat(tokens, 2, axis=0)
    padded = jnp.concatenate([repeated, jnp.zeros((1, D), jnp.bfloat16)], axis=0)
    row_limit = N_EXPERT * N_DP * CAP

    def one_expert(outputs, inputs):
        gate_matrix, up_matrix, down_matrix, number = inputs
        (row_where,) = jnp.nonzero(physical == number, size=row_limit, fill_value=total_rows)
        result = expert_forward(padded[row_where], gate_matrix, up_matrix, down_matrix)
        return outputs.at[row_where].set(result), None

    start_rows = jnp.zeros((total_rows + 1, D), jnp.bfloat16)
    numbers = jnp.arange(EXPERTS, dtype=jnp.int32)
    outputs, unused = lax.scan(one_expert, start_rows, (w_gate, w_up, w_down, numbers))
    picked = outputs[:total_rows].reshape(-1, 2, D).astype(jnp.float32)
    gate_real = gate_codes.astype(jnp.float32)
    weights = gate_real / jnp.sum(gate_real, axis=1, keepdims=True)
    return jnp.sum(weights[:, :, None] * picked, axis=1).astype(jnp.bfloat16)
```

```python
import jax
import jax.numpy as jnp
from jax import lax
from jax.sharding import PartitionSpec as P

HOT = 2
SLOTS = 4
Y = 4


def along_y(block, step):
    pairs = [(j, (j // Y) * Y + (j % Y + step) % Y) for j in range(2 * Y)]
    return lax.ppermute(block, "dp", pairs)


def across_x(block):
    return lax.ppermute(block, "dp", [(j, (j + Y) % (2 * Y)) for j in range(2 * Y)])


def cat(blocks):
    return jnp.concatenate(blocks, axis=0)


def add(*terms):
    total = terms[0].astype(jnp.float32)
    for term in terms[1:]:
        total = total + term.astype(jnp.float32)
    return total.astype(jnp.bfloat16)


def gather_y(block):
    half = block.shape[0] // 2
    one, three = along_y(block, 1), along_y(block, 3)
    low, high = along_y(one[:half], 1), along_y(three[half:], 3)
    return [one, cat([low, high]), three]


def scatter_y(own, one, two, three):
    half = own.shape[0] // 2
    low, high = along_y(two[:half], 3), along_y(two[half:], 1)
    one = cat([add(one[:half], low), one[half:]])
    three = cat([three[:half], add(three[half:], high)])
    return add(own, along_y(one, 3), along_y(three, 1))


def hidden_slice(rows, gate, up, down):
    gate_value = jnp.dot(rows, gate, preferred_element_type=jnp.float32)
    up_value = jnp.dot(rows, up, preferred_element_type=jnp.float32)
    hidden = (jax.nn.silu(gate_value) * up_value).astype(jnp.bfloat16)
    return jnp.dot(hidden, down, preferred_element_type=jnp.float32).astype(jnp.bfloat16)


def expert_block(rows, gate, up, down):
    total = rows.shape[0]
    na = (total * 3 // 8) // 16 * 16
    nb = total - na
    part_a, part_b = rows[:na], rows[na:]
    other_b = across_x(part_b)
    ring_a = [part_a] + gather_y(part_a)
    block_a = cat(ring_a)
    block_a, other_b = lax.optimization_barrier((block_a, other_b))
    other_a = across_x(block_a)
    block_b = cat([part_b, other_b])
    ring_b = gather_y(block_b)
    early = hidden_slice(cat([block_a, block_b]), gate, up, down)
    late = hidden_slice(cat([other_a] + ring_b), gate, up, down)
    back_a = across_x(late[: 4 * na])
    late_b = [late[4 * na + 2 * nb * k : 4 * na + 2 * nb * (k + 1)] for k in range(3)]
    sum_b = scatter_y(early[4 * na :], *late_b)
    back_b = across_x(sum_b[nb:])
    sum_a = add(early[: 4 * na], back_a)
    sum_a = scatter_y(*[sum_a[na * k : na * (k + 1)] for k in range(4)])
    return cat([sum_a, add(sum_b[:nb], back_b)])


def per_device(tokens, expert_ids, gate_codes, expert_order, w_gate, w_up, w_down):
    n_experts = lax.axis_size("expert")
    width = tokens.shape[1]
    main = n_experts * SLOTS
    gate_real = gate_codes.astype(jnp.float32)
    weights = gate_real / jnp.sum(gate_real, axis=1, keepdims=True)
    chosen = expert_ids.reshape(-1)
    place = jnp.arange(chosen.shape[0], dtype=jnp.int32)
    earlier = (chosen[None, :] == chosen[:, None]) & (place[None, :] < place[:, None])
    rank = jnp.sum(earlier.astype(jnp.int32), axis=1)
    experts = jnp.arange(n_experts, dtype=jnp.int32)
    physical = jnp.sum(
        jnp.where(chosen[:, None] == experts[None, :], expert_order[None, :], 0), axis=1
    )
    slot = (physical * 2 * SLOTS + rank).reshape(-1, 2)
    slots = jnp.arange(2 * main, dtype=jnp.int32)
    pick = (slot[:, :, None] == slots[None, None, :]).astype(jnp.bfloat16)
    send = lax.dot_general(
        pick[:, 0] + pick[:, 1], tokens, (((0,), (0,)), ((), ())),
        preferred_element_type=jnp.float32,
    ).astype(jnp.bfloat16)
    received = lax.all_to_all(
        send.reshape(n_experts, 2 * SLOTS, width), "expert", split_axis=0, concat_axis=0, tiled=True
    )
    me = lax.axis_index("expert")
    popular = (expert_order[0] == me) | (expert_order[1] == me)
    gate, up, down = w_gate[0], w_up[0], w_down[0]

    def many(rows):
        return expert_block(rows.reshape(2 * main, width), gate, up, down).reshape(rows.shape)

    def few(rows):
        done = expert_block(rows[:, :SLOTS].reshape(main, width), gate, up, down)
        done = done.reshape(n_experts, SLOTS, width)
        return jnp.concatenate([done, jnp.zeros_like(done)], axis=1)

    summed = lax.cond(popular, many, few, received)
    returned = lax.all_to_all(summed, "expert", split_axis=0, concat_axis=0, tiled=True)
    returned = returned.reshape(2 * main, width)
    mixed = jnp.zeros(tokens.shape, jnp.float32)
    for k in range(2):
        out = jnp.dot(pick[:, k], returned, preferred_element_type=jnp.float32)
        mixed = mixed + weights[:, k : k + 1] * out
    return mixed.astype(jnp.bfloat16)


def solution(mesh):
    in_specs = (
        P(("expert", "dp"), None),
        P(("expert", "dp"), None),
        P(("expert", "dp"), None),
        P(),
        P("expert", None, "dp"),
        P("expert", None, "dp"),
        P("expert", "dp", None),
    )
    return jax.shard_map(
        per_device, mesh=mesh, in_specs=in_specs, out_specs=P(("expert", "dp"), None), check_vma=False
    )
```

```python
import functools

import jax
import jax.numpy as jnp
from jax import lax
from jax.experimental import pallas as pl
from jax.experimental.pallas import tpu as pltpu
from jax.sharding import PartitionSpec as P

HOT = 2
SLOTS = 4
Y = 4


def along_y(block, step):
    pairs = [(j, (j // Y) * Y + (j % Y + step) % Y) for j in range(2 * Y)]
    return lax.ppermute(block, "dp", pairs)


def across_x(block):
    return lax.ppermute(block, "dp", [(j, (j + Y) % (2 * Y)) for j in range(2 * Y)])


def cat(blocks):
    return jnp.concatenate(blocks, axis=0)


def add(*terms):
    total = terms[0].astype(jnp.float32)
    for term in terms[1:]:
        total = total + term.astype(jnp.float32)
    return total.astype(jnp.bfloat16)


def expert_kernel(shape, *refs):
    count = sum(shape)
    rows, (gate, up, down), outs = refs[:count], refs[count : count + 3], refs[count + 3 : 2 * count + 3]
    gate_here, up_here, down_here, done = refs[2 * count + 3 :]
    copies = [
        pltpu.make_async_copy(there, here, done.at[k])
        for k, (there, here) in enumerate(((gate, gate_here), (up, up_here), (down, down_here)))
    ]
    for copy in copies:
        copy.start()
    first = 0
    for group, size in enumerate(shape):
        members = range(first, first + size)
        block = cat([rows[k][...] for k in members]) if size > 1 else rows[first][...]
        if group == 0:
            copies[0].wait()
        gate_value = jnp.dot(block, gate_here[...], preferred_element_type=jnp.float32)
        if group == 0:
            copies[1].wait()
        up_value = jnp.dot(block, up_here[...], preferred_element_type=jnp.float32)
        hidden = (gate_value / (1.0 + jnp.exp(-gate_value)) * up_value).astype(jnp.bfloat16)
        if group == 0:
            copies[2].wait()
        result = jnp.dot(hidden, down_here[...], preferred_element_type=jnp.float32)
        result = result.astype(jnp.bfloat16)
        start = 0
        for k in members:
            outs[k][...] = result[start : start + rows[k].shape[0]]
            start += rows[k].shape[0]
        first += size


def hidden_slice(groups, gate, up, down):
    blocks = [block for group in groups for block in group]
    total = sum(block.shape[0] for block in blocks)
    anywhere = pl.BlockSpec(memory_space=pl.ANY)
    near = pl.BlockSpec(memory_space=pltpu.VMEM)
    outs = pl.pallas_call(
        functools.partial(expert_kernel, tuple(len(group) for group in groups)),
        out_shape=[jax.ShapeDtypeStruct(block.shape, block.dtype) for block in blocks],
        in_specs=[near] * len(blocks) + [anywhere] * 3,
        out_specs=[near] * len(blocks),
        scratch_shapes=[
            pltpu.VMEM(gate.shape, gate.dtype),
            pltpu.VMEM(up.shape, up.dtype),
            pltpu.VMEM(down.shape, down.dtype),
            pltpu.SemaphoreType.DMA((3,)),
        ],
        compiler_params=pltpu.CompilerParams(vmem_limit_bytes=32 * 2**20),
        cost_estimate=pl.CostEstimate(flops=total, bytes_accessed=total, transcendentals=0),
    )(*blocks, gate, up, down)
    return outs


def expert_block(rows, gate, up, down):
    total = rows.shape[0]
    na = (total * 7 // 16) // 16 * 16
    nb = total - na
    part_a, part_b = rows[:na], rows[na:]
    other_b = across_x(part_b)
    half = na // 2
    one_a, three_a = along_y(part_a, 1), along_y(part_a, 3)
    low_a, high_a = along_y(one_a[:half], 1), along_y(three_a[half:], 3)
    near_a = cat([part_a, one_a, three_a])
    near_a, _ = lax.optimization_barrier((near_a, other_b))
    other_a = across_x(near_a)
    block_b = cat([part_b, other_b])
    one_b, three_b = along_y(block_b, 1), along_y(block_b, 3)
    sum_a, sum_b = hidden_slice([[near_a], [block_b]], gate, up, down)
    far_a = cat([low_a, high_a])
    one_b, three_b, far_a, sum_a, sum_b = lax.optimization_barrier(
        (one_b, three_b, far_a, sum_a, sum_b)
    )
    low_b, high_b = along_y(one_b[:nb], 1), along_y(three_b[nb:], 3)
    other_far = across_x(far_a)
    (other_a,) = hidden_slice([[other_a]], gate, up, down)
    low_b, high_b, _ = lax.optimization_barrier((low_b, high_b, other_a))
    low_b, high_b = hidden_slice([[low_b, high_b]], gate, up, down)
    one_b, three_b, far_a, other_far, _ = lax.optimization_barrier(
        (one_b, three_b, far_a, other_far, low_b)
    )
    one_b, three_b, far_a, other_far = hidden_slice(
        [[one_b], [three_b], [far_a, other_far]], gate, up, down
    )
    low_b, high_b = along_y(low_b, 3), along_y(high_b, 1)
    one_b = cat([add(one_b[:nb], low_b), one_b[nb:]])
    three_b = cat([three_b[:nb], add(three_b[nb:], high_b)])
    one_b, three_b = along_y(one_b, 3), along_y(three_b, 1)
    far_a = add(far_a, across_x(other_far))
    low_a, high_a = along_y(far_a[:half], 3), along_y(far_a[half:], 1)
    sum_a = add(sum_a, across_x(other_a))
    one_a, three_a = sum_a[na : 2 * na], sum_a[2 * na :]
    one_a = cat([add(one_a[:half], low_a), one_a[half:]])
    three_a = cat([three_a[:half], add(three_a[half:], high_a)])
    sum_b = add(sum_b, one_b, three_b)
    back_b = across_x(sum_b[nb:])
    sum_a = add(sum_a[:na], along_y(one_a, 3), along_y(three_a, 1))
    return cat([sum_a, add(sum_b[:nb], back_b)])


def per_device(tokens, expert_ids, gate_codes, expert_order, w_gate, w_up, w_down):
    n_experts = lax.axis_size("expert")
    width = tokens.shape[1]
    main = n_experts * SLOTS
    gate_real = gate_codes.astype(jnp.float32)
    weights = gate_real / jnp.sum(gate_real, axis=1, keepdims=True)
    chosen = expert_ids.reshape(-1)
    place = jnp.arange(chosen.shape[0], dtype=jnp.int32)
    earlier = (chosen[None, :] == chosen[:, None]) & (place[None, :] < place[:, None])
    rank = jnp.sum(earlier.astype(jnp.int32), axis=1)
    experts = jnp.arange(n_experts, dtype=jnp.int32)
    physical = jnp.sum(
        jnp.where(chosen[:, None] == experts[None, :], expert_order[None, :], 0), axis=1
    )
    slot = (physical * 2 * SLOTS + rank).reshape(-1, 2)
    slots = jnp.arange(2 * main, dtype=jnp.int32)
    pick = (slot[:, :, None] == slots[None, None, :]).astype(jnp.bfloat16)
    send = lax.dot_general(
        pick[:, 0] + pick[:, 1], tokens, (((0,), (0,)), ((), ())),
        preferred_element_type=jnp.float32,
    ).astype(jnp.bfloat16)
    received = lax.all_to_all(
        send.reshape(n_experts, 2 * SLOTS, width), "expert", split_axis=0, concat_axis=0, tiled=True
    )
    me = lax.axis_index("expert")
    popular = (expert_order[0] == me) | (expert_order[1] == me)
    gate, up, down = w_gate[0], w_up[0], w_down[0]

    def many(rows):
        return expert_block(rows.reshape(2 * main, width), gate, up, down).reshape(rows.shape)

    def few(rows):
        done = expert_block(rows[:, :SLOTS].reshape(main, width), gate, up, down)
        done = done.reshape(n_experts, SLOTS, width)
        return jnp.concatenate([done, jnp.zeros_like(done)], axis=1)

    summed = lax.cond(popular, many, few, received)
    returned = lax.all_to_all(summed, "expert", split_axis=0, concat_axis=0, tiled=True)
    returned = returned.reshape(2 * main, width)
    mixed = jnp.zeros(tokens.shape, jnp.float32)
    for k in range(2):
        out = jnp.dot(pick[:, k], returned, preferred_element_type=jnp.float32)
        mixed = mixed + weights[:, k : k + 1] * out
    return mixed.astype(jnp.bfloat16)


def solution(mesh):
    in_specs = (
        P(("expert", "dp"), None),
        P(("expert", "dp"), None),
        P(("expert", "dp"), None),
        P(),
        P("expert", None, "dp"),
        P("expert", None, "dp"),
        P("expert", "dp", None),
    )
    return jax.shard_map(
        per_device, mesh=mesh, in_specs=in_specs, out_specs=P(("expert", "dp"), None), check_vma=False
    )
```

```python
import functools

import jax
import jax.numpy as jnp
from jax import lax
from jax.experimental import pallas as pl
from jax.experimental.pallas import tpu as pltpu
from jax.sharding import PartitionSpec as P

HOT = 2
SLOTS = 4
Y = 4


def along_y(block, step):
    pairs = [(j, (j // Y) * Y + (j % Y + step) % Y) for j in range(2 * Y)]
    return lax.ppermute(block, "dp", pairs)


def across_x(block):
    return lax.ppermute(block, "dp", [(j, (j + Y) % (2 * Y)) for j in range(2 * Y)])


def cat(blocks):
    return jnp.concatenate(blocks, axis=0)


def add(*terms):
    total = terms[0].astype(jnp.float32)
    for term in terms[1:]:
        total = total + term.astype(jnp.float32)
    return total.astype(jnp.bfloat16)


def expert_kernel(shape, *refs):
    count = sum(shape)
    rows, (gate, up, down), outs = refs[:count], refs[count : count + 3], refs[count + 3 : 2 * count + 3]
    gate_here, up_here, down_here, done = refs[2 * count + 3 :]
    copies = [
        pltpu.make_async_copy(there, here, done.at[k])
        for k, (there, here) in enumerate(((gate, gate_here), (up, up_here), (down, down_here)))
    ]
    for copy in copies:
        copy.start()
    first = 0
    for group, size in enumerate(shape):
        members = range(first, first + size)
        block = cat([rows[k][...] for k in members]) if size > 1 else rows[first][...]
        if group == 0:
            copies[0].wait()
        gate_value = jnp.dot(block, gate_here[...], preferred_element_type=jnp.float32)
        if group == 0:
            copies[1].wait()
        up_value = jnp.dot(block, up_here[...], preferred_element_type=jnp.float32)
        hidden = (gate_value / (1.0 + jnp.exp(-gate_value)) * up_value).astype(jnp.bfloat16)
        if group == 0:
            copies[2].wait()
        result = jnp.dot(hidden, down_here[...], preferred_element_type=jnp.float32)
        result = result.astype(jnp.bfloat16)
        start = 0
        for k in members:
            outs[k][...] = result[start : start + rows[k].shape[0]]
            start += rows[k].shape[0]
        first += size


def hidden_slice(groups, gate, up, down):
    blocks = [block for group in groups for block in group]
    total = sum(block.shape[0] for block in blocks)
    anywhere = pl.BlockSpec(memory_space=pl.ANY)
    near = pl.BlockSpec(memory_space=pltpu.VMEM)
    outs = pl.pallas_call(
        functools.partial(expert_kernel, tuple(len(group) for group in groups)),
        out_shape=[jax.ShapeDtypeStruct(block.shape, block.dtype) for block in blocks],
        in_specs=[near] * len(blocks) + [anywhere] * 3,
        out_specs=[near] * len(blocks),
        scratch_shapes=[
            pltpu.VMEM(gate.shape, gate.dtype),
            pltpu.VMEM(up.shape, up.dtype),
            pltpu.VMEM(down.shape, down.dtype),
            pltpu.SemaphoreType.DMA((3,)),
        ],
        compiler_params=pltpu.CompilerParams(vmem_limit_bytes=32 * 2**20),
        cost_estimate=pl.CostEstimate(flops=total, bytes_accessed=total, transcendentals=0),
    )(*blocks, gate, up, down)
    return outs


def expert_block(rows, gate, up, down):
    total = rows.shape[0]
    na = total // 2
    nb = total - na
    part_a, part_b = rows[:na], rows[na:]
    other_b = across_x(part_b)
    half = na // 2
    one_a, three_a = along_y(part_a, 1), along_y(part_a, 3)
    low_a, high_a = along_y(one_a[:half], 1), along_y(three_a[half:], 3)
    near_a = cat([part_a, one_a, three_a])
    near_a, _ = lax.optimization_barrier((near_a, other_b))
    other_a = across_x(near_a)
    block_b = cat([part_b, other_b])
    one_b, three_b = along_y(block_b, 1), along_y(block_b, 3)
    sum_a, sum_b = hidden_slice([[near_a], [block_b]], gate, up, down)
    far_a = cat([low_a, high_a])
    one_b, three_b, far_a, sum_a, sum_b = lax.optimization_barrier(
        (one_b, three_b, far_a, sum_a, sum_b)
    )
    low_b, high_b = along_y(one_b[:nb], 1), along_y(three_b[nb:], 3)
    other_far = across_x(far_a)
    (other_a,) = hidden_slice([[other_a]], gate, up, down)
    low_b, high_b, _ = lax.optimization_barrier((low_b, high_b, other_a))
    low_b, high_b = hidden_slice([[low_b, high_b]], gate, up, down)
    one_b, three_b, far_a, other_far, _ = lax.optimization_barrier(
        (one_b, three_b, far_a, other_far, low_b)
    )
    one_b, three_b, far_a, other_far = hidden_slice(
        [[one_b], [three_b], [far_a, other_far]], gate, up, down
    )
    low_b, high_b = along_y(low_b, 3), along_y(high_b, 1)
    one_b = cat([add(one_b[:nb], low_b), one_b[nb:]])
    three_b = cat([three_b[:nb], add(three_b[nb:], high_b)])
    one_b, three_b = along_y(one_b, 3), along_y(three_b, 1)
    far_a = add(far_a, across_x(other_far))
    low_a, high_a = along_y(far_a[:half], 3), along_y(far_a[half:], 1)
    sum_a = add(sum_a, across_x(other_a))
    one_a, three_a = sum_a[na : 2 * na], sum_a[2 * na :]
    one_a = cat([add(one_a[:half], low_a), one_a[half:]])
    three_a = cat([three_a[:half], add(three_a[half:], high_a)])
    sum_b = add(sum_b, one_b, three_b)
    back_b = across_x(sum_b[nb:])
    sum_a = add(sum_a[:na], along_y(one_a, 3), along_y(three_a, 1))
    return cat([sum_a, add(sum_b[:nb], back_b)])


def per_device(tokens, expert_ids, gate_codes, expert_order, w_gate, w_up, w_down):
    n_experts = lax.axis_size("expert")
    width = tokens.shape[1]
    main = n_experts * SLOTS
    gate_real = gate_codes.astype(jnp.float32)
    weights = gate_real / jnp.sum(gate_real, axis=1, keepdims=True)
    chosen = expert_ids.reshape(-1)
    place = jnp.arange(chosen.shape[0], dtype=jnp.int32)
    earlier = (chosen[None, :] == chosen[:, None]) & (place[None, :] < place[:, None])
    rank = jnp.sum(earlier.astype(jnp.int32), axis=1)
    experts = jnp.arange(n_experts, dtype=jnp.int32)
    physical = jnp.sum(
        jnp.where(chosen[:, None] == experts[None, :], expert_order[None, :], 0), axis=1
    )
    slot = (physical * 2 * SLOTS + rank).reshape(-1, 2)
    slots = jnp.arange(2 * main, dtype=jnp.int32)
    pick = (slot[:, :, None] == slots[None, None, :]).astype(jnp.bfloat16)
    send = lax.dot_general(
        pick[:, 0] + pick[:, 1], tokens, (((0,), (0,)), ((), ())),
        preferred_element_type=jnp.float32,
    ).astype(jnp.bfloat16)
    received = lax.all_to_all(
        send.reshape(n_experts, 2 * SLOTS, width), "expert", split_axis=0, concat_axis=0, tiled=True
    )
    me = lax.axis_index("expert")
    popular = (expert_order[0] == me) | (expert_order[1] == me)
    gate, up, down = w_gate[0], w_up[0], w_down[0]

    def many(rows):
        return expert_block(rows.reshape(2 * main, width), gate, up, down).reshape(rows.shape)

    def few(rows):
        done = expert_block(rows[:, :SLOTS].reshape(main, width), gate, up, down)
        done = done.reshape(n_experts, SLOTS, width)
        return jnp.concatenate([done, jnp.zeros_like(done)], axis=1)

    summed = lax.cond(popular, many, few, received)
    returned = lax.all_to_all(summed, "expert", split_axis=0, concat_axis=0, tiled=True)
    returned = returned.reshape(2 * main, width)
    mixed = jnp.zeros(tokens.shape, jnp.float32)
    for k in range(2):
        out = jnp.dot(pick[:, k], returned, preferred_element_type=jnp.float32)
        mixed = mixed + weights[:, k : k + 1] * out
    return mixed.astype(jnp.bfloat16)


def solution(mesh):
    in_specs = (
        P(("expert", "dp"), None),
        P(("expert", "dp"), None),
        P(("expert", "dp"), None),
        P(),
        P("expert", None, "dp"),
        P("expert", None, "dp"),
        P("expert", "dp", None),
    )
    return jax.shard_map(
        per_device, mesh=mesh, in_specs=in_specs, out_specs=P(("expert", "dp"), None), check_vma=False
    )
```
